32 devices in a mesh: rows: 2 (over core), cols: 16 (over z, y, x).
Axes of the slice: x: 2, y: 2, z: 4, core: 2. Of those that a mesh axis runs over, the one named last changes fastest.
Arguments:
- jacobian: float32 [32768, 16384], P('rows', 'cols'), may hold values from -0.046875 to 0.046875
- targets: float32 [64, 32768], P(None, 'rows'), may hold values from 0 to 1
- anchor: float32 [64, 16384], P(None, 'cols'), may hold values from -6 to 6
- precision: float32 [16384], P('cols'), may hold values from 0.3 to 3
Outputs:
- samples: float32 [64, 16384], P(None, 'cols')
The draws below stay inside these ranges and needn't reach their ends.
All inputs are finite; a program needn't handle non-finite values.
Results may differ from the reference program's by a relative error of at most 0.0001.
Values sent between devices are 32-bit elements; how exact they have to be, the bound alone decides.
A program may use at most 128 MiB of HBM per device.

```python
import math
import jax
import jax.numpy as jnp
from jax import lax

PARAMS = 16384
SAMPLES = 64
STEPS = 3
ROWS = 32768


def block_scale(rng, dims, cuts, least, top_value):
    level, own = 1.0, jax.random.fold_in(rng, 6)
    for axis_at, shards_of in cuts:
        heights = jnp.exp(jax.random.uniform(jax.random.fold_in(own, axis_at), (shards_of,), jnp.float32, least / len(cuts), top_value / len(cuts)))
        level = level * jnp.repeat(heights, dims[axis_at] // shards_of).reshape([-1 if axis == axis_at else 1 for axis in range(len(dims))])
    return level


def gaussian(stream_key, extent, scale, limit, cuts=(), dtype=jnp.bfloat16):
    values = jax.random.normal(stream_key, extent, jnp.float32) * scale
    if len(cuts) > 0:
        values = block_scale(stream_key, extent, cuts, -0.22, 0.18) * values
    return jnp.clip(values, min=-limit, max=limit).astype(dtype)


def setup_inputs(seed: int = 0) -> dict:
    splits = jax.random.split(jax.random.key(seed), 5)
    jacobian = gaussian(splits[0], (ROWS, PARAMS), PARAMS ** -0.5, 0.046875, ((0, 2), (1, 16)), jnp.float32)
    targets = jnp.clip(1.0 * jax.random.uniform(splits[1], (SAMPLES, ROWS), jnp.float32) ** block_scale(splits[1], (SAMPLES, ROWS), ((1, 2),), -0.2, 0.2), 0.0, 1.0)
    anchor = gaussian(splits[2], (SAMPLES, PARAMS), 1.0, 6.0, ((1, 16),), jnp.float32)
    precision = jnp.clip(jnp.exp(math.log(3.0) - 2.3025851 * jax.random.uniform(splits[3], (PARAMS,), jnp.float32) ** block_scale(splits[3], (PARAMS,), ((0, 16),), -0.2, 0.2)), 0.3, 3.0)
    return dict(jacobian=jacobian, targets=targets, anchor=anchor, precision=precision)


def reference(jacobian, targets, anchor, precision):
    clip_level = 0.2 * math.sqrt(ROWS / PARAMS)
    theta = anchor
    velocity = jnp.zeros_like(anchor)
    for step in range(STEPS):
        logits = lax.dot_general(theta, jacobian, (((1,), (1,)), ((), ())), precision=lax.Precision.HIGHEST, preferred_element_type=jnp.float32)
        residual = jax.nn.sigmoid(logits) - targets
        gradient = jnp.dot(residual, jacobian, precision=lax.Precision.HIGHEST, preferred_element_type=jnp.float32)
        gradient = gradient + precision[None, :] * (theta - anchor)
        rms_value = jnp.sqrt(lax.optimization_barrier(jnp.sum(gradient * gradient, axis=1)) / PARAMS + 1e-06)
        scale = jnp.minimum(1.0, clip_level / rms_value)
        velocity = 0.9 * velocity + scale[:, None] * gradient
        theta = theta - 0.5 * velocity
    return theta
```

```python
import math

import jax
import jax.numpy as jnp
from jax import lax
from jax.sharding import PartitionSpec as P

STEPS = 3
CHUNKS = 4


def swap(value, rows, cols, partner_of):
    pairs = []
    for row in range(rows):
        for col in range(cols):
            to_row, to_col = partner_of(row, col)
            pairs.append((row * cols + col, to_row * cols + to_col))
    return lax.ppermute(value, ("rows", "cols"), pairs)


def body(jacobian, targets, anchor, precision):
    rows, cols = lax.axis_size("rows"), lax.axis_size("cols")
    row_dev, col_dev = jacobian.shape
    total_params = col_dev * cols
    clip_level = 0.2 * math.sqrt(row_dev * rows / total_params)
    bits = cols.bit_length() - 1
    row_bits = rows.bit_length() - 1
    row_at, col_at = lax.axis_index("rows"), lax.axis_index("cols")
    lead = max(1, bits // 4)
    orders = []
    for row in range(rows):
        first = list(range(bits))
        if row % 2:
            first = first[lead : 2 * lead] + first[:lead] + first[2 * lead :]
        orders.append(first)

    def mine(stage):
        bit = jnp.asarray([order[stage] for order in orders], jnp.int32)[row_at]
        return (col_at >> bit) & 1

    def cross(value, stage):
        return swap(value, rows, cols, lambda r, c: (r, c ^ (1 << orders[r][stage])))

    width = row_dev // CHUNKS
    sides = [mine(stage) for stage in range(bits)]

    def reduce_scatter(block):
        for stage in range(bits):
            half = block.shape[1] // 2
            kept = lax.dynamic_slice_in_dim(block, sides[stage] * half, half, 1)
            sent = lax.dynamic_slice_in_dim(block, (1 - sides[stage]) * half, half, 1)
            block = kept + cross(sent, stage)
        return block

    def all_gather(block):
        for stage in reversed(range(bits)):
            other = cross(block, stage)
            low = jnp.where(sides[stage] == 0, block, other)
            high = jnp.where(sides[stage] == 0, other, block)
            block = jnp.concatenate([low, high], axis=1)
        return block

    share = width >> bits
    within = 0
    for stage in range(bits):
        within = within + sides[stage] * (width >> (stage + 1))
    targets_own = [
        lax.dynamic_slice_in_dim(targets, index * width + within, share, 1)
        for index in range(CHUNKS)
    ]
    blocks = [jacobian[index * width : (index + 1) * width] for index in range(CHUNKS)]

    theta = anchor
    velocity = jnp.zeros_like(anchor)
    for step in range(STEPS):
        gradient = precision[None, :] * (theta - anchor)
        residuals = []
        for index in range(CHUNKS):
            part_logits = lax.dot_general(
                theta,
                blocks[index],
                (((1,), (1,)), ((), ())),
                precision=lax.Precision.HIGH,
                preferred_element_type=jnp.float32,
            )
            logits = reduce_scatter(part_logits)
            residuals.append(all_gather(jax.nn.sigmoid(logits) - targets_own[index]))
        total = 0.0
        for index in range(CHUNKS):
            total = total + jnp.dot(
                residuals[index],
                blocks[index],
                precision=lax.Precision.HIGH,
                preferred_element_type=jnp.float32,
            )
        for bit in range(row_bits):
            total = total + swap(total, rows, cols, lambda r, c: (r ^ (1 << bit), c))
        gradient = total + gradient
        squares = jnp.sum(gradient * gradient, axis=1)[None, :]
        for bit in range(bits):
            squares = squares + swap(squares, rows, cols, lambda r, c: (r, c ^ (1 << bit)))
        scale = jnp.minimum(1.0, clip_level / jnp.sqrt(squares[0] / total_params + 1e-06))
        velocity = 0.9 * velocity + scale[:, None] * gradient
        theta = theta - 0.5 * velocity
    return theta


def solution(mesh):
    in_specs = (P("rows", "cols"), P(None, "rows"), P(None, "cols"), P("cols"))
    out_specs = P(None, "cols")
    return jax.shard_map(body, mesh=mesh, in_specs=in_specs, out_specs=out_specs, check_vma=False)
```

```python
import math

import jax
import jax.numpy as jnp
from jax import lax
from jax.experimental import pallas as pl
from jax.experimental.pallas import tpu as pltpu
from jax.sharding import PartitionSpec as P

STEPS = 3
CHUNKS = 4
TILE = 512
VMEM_LIMIT = 40 << 20


def split(value):
    high = value.astype(jnp.bfloat16)
    low = (value - high.astype(jnp.float32)).astype(jnp.bfloat16)
    return high, low


def logits_kernel(theta_ref, jacobian_ref, out_ref):
    samples = theta_ref.shape[0]
    weights = jnp.concatenate(split(theta_ref[...]), axis=0)
    high, low = split(jacobian_ref[...])
    contract = (((1,), (1,)), ((), ()))
    both = lax.dot_general(high, weights, contract, preferred_element_type=jnp.float32)
    both += lax.dot_general(low, weights, contract, preferred_element_type=jnp.float32)
    both = both.T
    out_ref[...] = both[:samples] + both[samples:]


def gradient_kernel(residual_ref, jacobian_ref, out_ref):
    samples = residual_ref.shape[0]
    left = jnp.concatenate(split(residual_ref[...]), axis=0)
    high, low = split(jacobian_ref[...])
    both = jnp.dot(left, high, preferred_element_type=jnp.float32)
    both += jnp.dot(left, low, preferred_element_type=jnp.float32)
    term = both[:samples] + both[samples:]

    @pl.when(pl.program_id(0) == 0)
    def _():
        out_ref[...] = term

    @pl.when(pl.program_id(0) > 0)
    def _():
        out_ref[...] += term


def on_rows(kernel, left, jacobian, index, width, reduce):
    samples, col_dev = left.shape[0], jacobian.shape[1]
    tile = math.gcd(TILE, width)
    tiles = width // tile
    moving = pl.BlockSpec((samples, tile), lambda at: (0, at))
    fixed = pl.BlockSpec((samples, col_dev), lambda at: (0, 0))
    return pl.pallas_call(
        kernel,
        grid=(tiles,),
        in_specs=[
            moving if reduce else fixed,
            pl.BlockSpec((tile, col_dev), lambda at: (index * tiles + at, 0)),
        ],
        out_specs=fixed if reduce else moving,
        out_shape=jax.ShapeDtypeStruct((samples, col_dev if reduce else width), jnp.float32),
        compiler_params=pltpu.CompilerParams(vmem_limit_bytes=VMEM_LIMIT),
        cost_estimate=pl.CostEstimate(
            flops=16 * samples * width * col_dev,
            bytes_accessed=4 * width * col_dev,
            transcendentals=0,
        ),
    )(left, jacobian)


def swap(value, rows, cols, partner_of):
    pairs = []
    for row in range(rows):
        for col in range(cols):
            to_row, to_col = partner_of(row, col)
            pairs.append((row * cols + col, to_row * cols + to_col))
    return lax.ppermute(value, ("rows", "cols"), pairs)


def body(jacobian, targets, anchor, precision):
    rows, cols = lax.axis_size("rows"), lax.axis_size("cols")
    row_dev, col_dev = jacobian.shape
    total_params = col_dev * cols
    clip_level = 0.2 * math.sqrt(row_dev * rows / total_params)
    bits = cols.bit_length() - 1
    row_bits = rows.bit_length() - 1
    row_at, col_at = lax.axis_index("rows"), lax.axis_index("cols")
    lead = max(1, bits // 4)
    orders = []
    for row in range(rows):
        first = list(range(bits))
        if row % 2:
            first = first[lead : 2 * lead] + first[:lead] + first[2 * lead :]
        orders.append(first)

    def mine(stage):
        bit = jnp.asarray([order[stage] for order in orders], jnp.int32)[row_at]
        return (col_at >> bit) & 1

    def cross(value, stage):
        return swap(value, rows, cols, lambda r, c: (r, c ^ (1 << orders[r][stage])))

    width = row_dev // CHUNKS
    sides = [mine(stage) for stage in range(bits)]

    def reduce_scatter(block):
        for stage in range(bits):
            half = block.shape[1] // 2
            kept = lax.dynamic_slice_in_dim(block, sides[stage] * half, half, 1)
            sent = lax.dynamic_slice_in_dim(block, (1 - sides[stage]) * half, half, 1)
            block = kept + cross(sent, stage)
        return block

    def all_gather(block):
        for stage in reversed(range(bits)):
            other = cross(block, stage)
            low = jnp.where(sides[stage] == 0, block, other)
            high = jnp.where(sides[stage] == 0, other, block)
            block = jnp.concatenate([low, high], axis=1)
        return block

    share = width >> bits
    within = 0
    for stage in range(bits):
        within = within + sides[stage] * (width >> (stage + 1))
    targets_own = [
        lax.dynamic_slice_in_dim(targets, index * width + within, share, 1)
        for index in range(CHUNKS)
    ]

    theta = anchor
    velocity = jnp.zeros_like(anchor)
    for step in range(STEPS):
        gradient = precision[None, :] * (theta - anchor)
        residuals = []
        for index in range(CHUNKS):
            part_logits = on_rows(logits_kernel, theta, jacobian, index, width, False)
            logits = reduce_scatter(part_logits)
            residuals.append(all_gather(jax.nn.sigmoid(logits) - targets_own[index]))
        total = 0.0
        for index in range(CHUNKS):
            total = total + on_rows(
                gradient_kernel, residuals[index], jacobian, index, width, True
            )
        for bit in range(row_bits):
            total = total + swap(total, rows, cols, lambda r, c: (r ^ (1 << bit), c))
        gradient = total + gradient
        squares = jnp.sum(gradient * gradient, axis=1)[None, :]
        for bit in range(bits):
            squares = squares + swap(squares, rows, cols, lambda r, c: (r, c ^ (1 << bit)))
        scale = jnp.minimum(1.0, clip_level / jnp.sqrt(squares[0] / total_params + 1e-06))
        velocity = 0.9 * velocity + scale[:, None] * gradient
        theta = theta - 0.5 * velocity
    return theta


def solution(mesh):
    in_specs = (P("rows", "cols"), P(None, "rows"), P(None, "cols"), P("cols"))
    out_specs = P(None, "cols")
    return jax.shard_map(body, mesh=mesh, in_specs=in_specs, out_specs=out_specs, check_vma=False)
```
